32 devices in a mesh: row: 4 (over y, x), col: 8 (over z, core).
Axes of the slice: x: 2, y: 2, z: 4, core: 2. Of those that a mesh axis runs over, the one named last changes fastest.
Arguments:
- object_field: float32 [2, 1536, 2048], P(None, 'row', 'col'), may hold values from -5 to 5
- probe_modes: float32 [2, 2, 256, 256], replicated, may hold values from -4 to 4
- scan_positions: int32 [4, 8, 2, 2], P('row', 'col'), may hold values from 0 to 256, as said below
- amplitudes: bfloat16 [4, 8, 2, 256, 256], P('row', 'col'), may hold values from 0.5 to 1.5
Outputs:
- object_out: float32 [2, 1536, 2048], P(None, 'row', 'col')
- probe_out: float32 [2, 2, 256, 256], replicated
The draws below stay inside these ranges and needn't reach their ends.
Inputs may be any that keep to these rules, and one draw needn't show every extreme that they name: `scan_positions`: in even batches the row offset is at most 128; in odd batches it is at least 192. The column offset lies in 32 to 128 in every batch. Every window lies inside its tile extended by 128 rows below and 128 columns to the right.
All inputs are finite; a program needn't handle non-finite values.
Results may differ from the reference program's by a relative error of at most 0.0003.
Values sent between devices are 32-bit elements; how exact they have to be, the bound alone decides.
A program may use at most 64 MiB of HBM per device.

```python
import math
import jax
import jax.numpy as jnp
from jax import lax

WIN = 256
MODES = 2
HALO = 128
TILE_R = 384
TILE_C = 256
BATCHES = 2
OUTER = 1
NY = 1536
NX = 2048
POS_ALL = 64
N_ROW = 4
N_COL = 8


def draw_scan_positions(key, part):
    key_rows = jax.random.fold_in(key, 11)
    key_cols = jax.random.fold_in(key, 23)
    lowest = jnp.array([0 if step % 2 == 0 else TILE_R + HALO - WIN - HALO // 2 for step in range(BATCHES)], jnp.int32)
    highest = jnp.array([TILE_R - WIN if step % 2 == 0 else TILE_R + HALO - WIN for step in range(BATCHES)], jnp.int32)
    rows = jax.random.randint(key_rows, (N_ROW, N_COL, BATCHES), lowest, highest + 1)
    cols = jax.random.randint(key_cols, (N_ROW, N_COL, BATCHES), HALO // 4, TILE_C + HALO - WIN + 1)
    rows = rows.at[0, 0, 0].set(0)
    rows = rows.at[0, 0, 1].set(TILE_R + HALO - WIN)
    cols = cols.at[0, 0, 0].set(HALO // 4)
    cols = cols.at[0, 0, 1].set(TILE_C + HALO - WIN)
    return jnp.stack([rows, cols], axis=-1).astype(jnp.int32)


def block_levels(key, shape, pieces, least, high):
    def one(axis_at, parts):
        draws = jax.random.uniform(jax.random.fold_in(jax.random.fold_in(key, 6), axis_at), (parts,), jnp.float32, least / len(pieces), high / len(pieces))
        return jnp.repeat(jnp.exp(draws), shape[axis_at] // parts).reshape((-1,) + (1,) * (len(shape) - axis_at - 1))

    factor_of = one(*pieces[0])
    for cut in pieces[1:]:
        factor_of = factor_of * one(*cut)
    return factor_of


def centred(key, dims, width, limit, split=(), held_as=jnp.bfloat16):
    result = width * jax.random.normal(key, dims, jnp.float32)
    if split:
        result = result * block_levels(key, dims, split, -0.22, 0.18)
    return jnp.clip(result, -limit, limit).astype(held_as)


def setup_inputs(seed: int = 0) -> dict:
    key_list = jax.random.split(jax.random.key(seed), 5)
    return {
        "object_field": centred(key_list[0], (2, NY, NX), 0.7, 5.0, ((1, 4), (2, 8)), jnp.float32),
        "probe_modes": centred(key_list[1], (MODES, 2, WIN, WIN), 0.5, 4.0, (), jnp.float32),
        "scan_positions": draw_scan_positions(jax.random.fold_in(key_list[4], 71), 0),
        "amplitudes": jnp.clip(0.5 + 1.0 * jax.random.uniform(key_list[3], (N_ROW, N_COL, BATCHES, WIN, WIN), jnp.float32) ** block_levels(key_list[3], (N_ROW, N_COL, BATCHES, WIN, WIN), ((0, 4), (1, 8)), -0.2, 0.2), 0.5, 1.5).astype(jnp.bfloat16),
    }


def window_fit(window, probe_modes, amplitude):
    object_window = window[0] + 1j * window[1]
    probe_complex = probe_modes[:, 0] + 1j * probe_modes[:, 1]
    wave = probe_complex * object_window
    far_field = jnp.fft.fft2(wave, norm='ortho')
    intensity = lax.optimization_barrier(jnp.sum(far_field.real ** 2 + far_field.imag ** 2, axis=0))
    factor = amplitude / jnp.sqrt(jnp.maximum(intensity, 0.1)) - 1.0
    chi_field = jnp.fft.ifft2(far_field * factor, norm='ortho')
    object_grad = lax.optimization_barrier(jnp.sum(jnp.conj(probe_complex) * chi_field, axis=0))
    probe_grad = jnp.conj(object_window) * chi_field
    object_part = jnp.stack([object_grad.real, object_grad.imag], axis=0)
    probe_part = jnp.stack([probe_grad.real, probe_grad.imag], axis=1)
    return (object_part, probe_part)

def reference(object_field, probe_modes, scan_positions, amplitudes):
    for outer_step in range(OUTER):
        power = jnp.sum(probe_modes * probe_modes) / (WIN * WIN)
        update_step = 1.0 / (power + 1e-06)
        probe_sum = jnp.zeros_like(probe_modes)
        for batch_index in range(BATCHES):
            padded = jnp.pad(object_field, ((0, 0), (0, HALO), (0, HALO)))

            def visit(carry, flat_index, padded=padded, batch_index=batch_index):
                gradient, probe_acc = carry
                tile_row = (flat_index // N_COL).astype(jnp.int32)
                tile_col = (flat_index % N_COL).astype(jnp.int32)
                offsets = scan_positions[tile_row, tile_col, batch_index]
                row_start = (tile_row * TILE_R + offsets[0]).astype(jnp.int32)
                col_start = (tile_col * TILE_C + offsets[1]).astype(jnp.int32)
                anchor = (jnp.int32(0), row_start, col_start)
                window = lax.dynamic_slice(padded, anchor, (2, WIN, WIN))
                amplitude = amplitudes[tile_row, tile_col, batch_index].astype(jnp.float32)
                object_part, probe_part = window_fit(window, probe_modes, amplitude)
                current = lax.dynamic_slice(gradient, anchor, (2, WIN, WIN))
                gradient = lax.dynamic_update_slice(gradient, current + object_part, anchor)
                return ((gradient, probe_acc + probe_part), None)
            start = (jnp.zeros_like(padded), jnp.zeros_like(probe_modes))
            (gradient, probe_acc), _ = lax.scan(visit, start, jnp.arange(N_ROW * N_COL, dtype=jnp.int32))
            object_field = object_field + update_step * gradient[:, :NY, :NX]
            probe_sum = probe_sum + probe_acc
        probe_modes = probe_modes + probe_sum / math.sqrt(POS_ALL)
    return (object_field, probe_modes)
```

```python
import functools
import math

import jax
import jax.numpy as jnp
import numpy as np
from jax import lax
from jax.experimental import pallas as pl
from jax.experimental.pallas import tpu as pltpu
from jax.sharding import PartitionSpec as P

HALO = 128
ODD_LOW = 192
F32 = jnp.float32
BF16 = jnp.bfloat16
MESH = pl.DeviceIdType.MESH


def dft_tables(width):
    index = np.arange(width)
    angle = (index[:, None] * index[None, :] % width) * (2.0 * math.pi / width)
    out = []
    for table in (np.cos(angle) / math.sqrt(width), np.sin(angle) / math.sqrt(width)):
        table = table.astype(np.float32)
        high = table.astype(BF16)
        low = (table - high.astype(np.float32)).astype(BF16)
        out += [high, low]
    return np.stack(out)


def split(value):
    high = value.astype(BF16)
    return high, (value - high.astype(F32)).astype(BF16)


def dot3(a_hi, a_lo, b_hi, b_lo):
    dot = functools.partial(jnp.dot, preferred_element_type=F32)
    return dot(a_hi, b_hi) + (dot(a_hi, b_lo) + dot(a_lo, b_hi))


def kernel(
    n_row, n_col, reduce_here, divisor,
    pos, obj, probe, amps, tables, obj_out, probe_out,
    e0, gx, n1, e1, g1, zbuf, from_left, from_right, spill1, down_send, from_up,
    a_hi, a_lo, b_hi, b_lo, xs_hi, xs_lo, ls_hi, ls_lo, fbuf, wbuf,
    sbuf, core_in, tbuf, row_in, ubuf, z_in, gather, ssem, rsem,
):
    row = lax.axis_index("row")
    col = lax.axis_index("col")
    width = probe.shape[-1]
    tile_rows, tile_cols = obj.shape[1], obj.shape[2]
    odd_own = tile_rows - ODD_LOW
    core = lax.rem(col, 2)
    zed = col // 2
    n_zed = n_col // 2
    has_left, has_right = col > 0, col < n_col - 1
    has_up, has_down = row > 0, row < n_row - 1
    partner = (row, col + 1 - 2 * core)
    row_peers = [(lax.rem(row + k, n_row), col) for k in range(1, n_row)]
    z_peers = [(row, lax.rem(zed + k, n_zed) * 2 + core) for k in range(1, n_zed)]
    left, right = (row, col - 1), (row, col + 1)
    up, down = (row - 1, col), (row + 1, col)

    count = [0]
    pending = []

    def remote(src, dst, dev, sends=None, receives=None):
        i = count[0]
        count[0] += 1
        copy = pltpu.make_async_remote_copy(
            src_ref=src, dst_ref=dst, send_sem=ssem.at[i], recv_sem=rsem.at[i],
            device_id=dev, device_id_type=MESH)

        def start():
            if sends is None:
                copy.start()
            else:
                pl.when(sends)(copy.start)
            pending.append((sends, copy))

        def arrive():
            if receives is None:
                copy.wait_recv()
            else:
                pl.when(receives)(copy.wait_recv)

        return start, arrive

    barrier = pltpu.get_barrier_semaphore()
    beside = (row, lax.rem(col + 2 * core - 1 + n_col, n_col))
    greeted = [partner, beside] + row_peers + z_peers
    for dev in greeted:
        pl.semaphore_signal(barrier, inc=1, device_id=dev, device_id_type=MESH)
    pl.semaphore_wait(barrier, len(greeted))

    halo = slice(tile_cols, tile_cols + HALO)
    start, halo_arrives = remote(obj.at[:, :, 0:HALO], e0.at[:, 0:tile_rows, halo], left, has_left, has_right)
    start()

    e0[:, 0:tile_rows, 0:tile_cols] = obj[...]
    for hi, part in ((True, 0), (False, 1)):
        cosine, sine = tables[part], tables[2 + part]
        a, b = (a_hi, b_hi) if hi else (a_lo, b_lo)
        for i in (0, 1):
            a[pl.ds(i * width, width), pl.ds(i * width, width)] = cosine
            b[pl.ds(i * width, width), pl.ds(i * width, width)] = cosine
        a[0:width, width:] = sine
        a[width:, 0:width] = -sine
        b[0:width, width:] = -sine
        b[width:, 0:width] = sine
    power = jnp.sum(
        jnp.sum(probe[0, 0] ** 2 + probe[0, 1] ** 2 + probe[1, 0] ** 2 + probe[1, 1] ** 2,
                axis=0, keepdims=True), axis=1, keepdims=True) / (width * width)
    step = 1.0 / (power + 1e-06)

    @pl.when(jnp.logical_not(has_right))
    def _():
        e0[:, 0:tile_rows, halo] = jnp.zeros((2, tile_rows, HALO), F32)
        from_right[...] = jnp.zeros_like(from_right)

    @pl.when(jnp.logical_not(has_left))
    def _():
        from_left[...] = jnp.zeros_like(from_left)
        spill1[...] = jnp.zeros_like(spill1)

    @pl.when(jnp.logical_not(has_down))
    def _():
        e1[:, odd_own : odd_own + HALO, :] = jnp.zeros((2, HALO, tile_cols + HALO), F32)

    @pl.when(jnp.logical_not(has_up))
    def _():
        from_up[...] = jnp.zeros_like(from_up)

    def block(i):
        return slice(i * width, (i + 1) * width)

    def one_hot(shape, dim, shift):
        here = lax.broadcasted_iota(jnp.int32, shape, dim)
        other = lax.broadcasted_iota(jnp.int32, shape, 1 - dim)
        return jnp.where(here == other + shift, 1.0, 0.0).astype(BF16)

    def pick(value, row_table, col_table):
        dot = functools.partial(jnp.dot, preferred_element_type=F32)
        parts = [dot(row_table, part).astype(BF16) for part in split(value)]
        return dot(parts[0], col_table) + dot(parts[1], col_table)

    def fit(source, first_row, col_start, batch, after_mode):
        height, total_lanes = source.shape[1:]
        row_table = one_hot((width, height), 1, first_row)
        col_table = one_hot((total_lanes, width), 0, col_start)
        for p in (0, 1):
            wbuf[p] = pick(source[p], row_table, col_table)
        for m in (0, 1):
            pr, pi, wr, wi = probe[m, 0], probe[m, 1], wbuf[0], wbuf[1]
            xs_hi[block(m), block(0)], xs_lo[block(m), block(0)] = split(pr * wr - pi * wi)
            xs_hi[block(m), block(1)], xs_lo[block(m), block(1)] = split(pr * wi + pi * wr)
        for m in (0, 1):
            y = dot3(xs_hi[block(m), :], xs_lo[block(m), :], b_hi[...], b_lo[...])
            for p in (0, 1):
                ls_hi[block(p), block(m)], ls_lo[block(p), block(m)] = split(y[:, block(p)])
        for p in (0, 1):
            fbuf[p] = dot3(a_hi[block(p), :], a_lo[block(p), :], ls_hi[...], ls_lo[...])
        intensity = sum(fbuf[p, :, block(m)] ** 2 for p in (0, 1) for m in (0, 1))
        factor = amps[batch].astype(F32) * lax.rsqrt(jnp.maximum(intensity, 0.1)) - 1.0
        for p in (0, 1):
            for m in (0, 1):
                ls_hi[block(p), block(m)], ls_lo[block(p), block(m)] = split(
                    fbuf[p, :, block(m)] * factor)
        for p in (0, 1):
            h = dot3(b_hi[block(p), :], b_lo[block(p), :], ls_hi[...], ls_lo[...])
            for m in (0, 1):
                xs_hi[block(m), block(p)], xs_lo[block(m), block(p)] = split(h[:, block(m)])
        for m in (0, 1):
            chi = dot3(xs_hi[block(m), :], xs_lo[block(m), :], a_hi[...], a_lo[...])
            cr, ci = chi[:, block(0)], chi[:, block(1)]
            wr, wi = wbuf[0], wbuf[1]
            pr, pi = probe[m, 0], probe[m, 1]
            grad_r, grad_i = wr * cr + wi * ci, wr * ci - wi * cr
            gor, goi = (pr * cr + pi * ci) * step, (pr * ci - pi * cr) * step
            if batch == 0:
                sbuf[2 * m], sbuf[2 * m + 1] = grad_r, grad_i
            else:
                sbuf[2 * m] += grad_r
                sbuf[2 * m + 1] += grad_i
            if m == 0:
                zbuf[0], zbuf[1] = gor, goi
            else:
                zbuf[0] += gor
                zbuf[1] += goi
            after_mode(m)

    def place(target, offset, col_start):
        height, total_lanes = target.shape[1:]
        row_table = one_hot((height, width), 0, offset)
        col_table = one_hot((width, total_lanes), 1, col_start)
        for p in (0, 1):
            target[p] = pick(zbuf[p], row_table, col_table)

    halo_arrives()
    fit(e0, pos[0], pos[1], 0, lambda m: None)
    place(gx, pos[0], pos[1])

    top, rest, late = slice(0, HALO), slice(HALO, tile_rows), slice(ODD_LOW, tile_rows)
    edge, mid = slice(0, HALO), slice(HALO, tile_cols)
    below = slice(odd_own, odd_own + HALO)
    s_rt, a_rt = remote(gx.at[:, top, halo], from_left.at[:, top], right, has_right, has_left)
    s_lt, a_lt = remote(gx.at[:, top, edge], from_right.at[:, top], left, has_left, has_right)
    s_rr, a_rr = remote(gx.at[:, rest, halo], from_left.at[:, rest], right, has_right, has_left)
    s_lr, a_lr = remote(gx.at[:, late, edge], from_right.at[:, late], left, has_left, has_right)
    s_um, a_um = remote(n1.at[:, top, mid], e1.at[:, below, mid], up, has_up, has_down)
    s_ue, a_ue = remote(n1.at[:, top, edge], e1.at[:, below, edge], up, has_up, has_down)
    s_uh, a_uh = remote(n1.at[:, top, halo], e1.at[:, below, halo], up, has_up, has_down)
    s_rt()
    s_lt()
    s_rr()
    s_lr()
    n1[:, top, mid] = e0[:, top, mid] + gx[:, top, mid]
    s_um()
    n1[:, rest, mid] = e0[:, rest, mid] + gx[:, rest, mid]
    inside = jnp.where(has_right, 1.0, 0.0).astype(F32)
    a_rt()
    n1[:, top, edge] = e0[:, top, edge] + gx[:, top, edge] + from_left[:, top]
    s_ue()
    a_lt()
    n1[:, top, halo] = (e0[:, top, halo] + gx[:, top, halo] + from_right[:, top]) * inside
    s_uh()
    a_rr()
    n1[:, rest, edge] = e0[:, rest, edge] + gx[:, rest, edge] + from_left[:, rest]
    a_lr()
    e1[:, 0:odd_own, 0:tile_cols] = n1[:, late, 0:tile_cols]
    e1[:, 0:odd_own, halo] = (e0[:, late, halo] + gx[:, late, halo] + from_right[:, late]) * inside
    a_um()
    a_ue()
    a_uh()

    core_copies = [
        remote(sbuf.at[2 * m + 1 - core], core_in.at[m], partner)
        for m in (0, 1) if reduce_here]

    def after_mode(m):
        if reduce_here:
            core_copies[m][0]()

    fit(e1, pos[2] - ODD_LOW, pos[3], 1, after_mode)
    place(g1, pos[2] - ODD_LOW, pos[3])

    s_sb, a_sb = remote(g1.at[:, below, halo], spill1.at[:, below], right, has_right, has_left)
    s_so, a_so = remote(g1.at[:, 0:odd_own, halo], spill1.at[:, 0:odd_own], right, has_right, has_left)
    s_dm, a_dm = remote(g1.at[:, below, mid], from_up.at[:, :, mid], down, has_down, has_up)
    s_de, a_de = remote(down_send, from_up.at[:, :, edge], down, has_down, has_up)
    s_sb()
    s_so()

    def relay():
        s_dm()
        a_sb()
        down_send[...] = g1[:, below, edge] + spill1[:, below]
        s_de()

    if reduce_here:
        part = width // n_row
        piece = part // n_zed
        row_base = row * part
        z_base = row_base + zed * piece
        row_copies, z_copies = [], []
        for m in (0, 1):
            core_copies[m][1]()
            tbuf[m] = sbuf[2 * m + core] + core_in[m]
            group = [
                remote(tbuf.at[m, pl.ds(pl.multiple_of(dev[0] * part, 8), part)], row_in.at[m, k], dev)
                for k, dev in enumerate(row_peers)]
            for start, _ in group:
                start()
            row_copies.append(group)
        relay()
        for m in (0, 1):
            total = tbuf[m, pl.ds(pl.multiple_of(row_base, 8), part)]
            for k, (_, arrive) in enumerate(row_copies[m]):
                arrive()
                total = total + row_in[m, k]
            ubuf[m] = total
            group = [
                remote(ubuf.at[m, pl.ds(pl.multiple_of(dev[1] // 2 * piece, 8), piece)], z_in.at[m, k], dev)
                for k, dev in enumerate(z_peers)]
            for start, _ in group:
                start()
            z_copies.append(group)
        z_back, row_back, core_back = [], [], []
        own = pl.ds(pl.multiple_of(z_base, 8), piece)
        for m in (0, 1):
            total = ubuf[m, pl.ds(pl.multiple_of(zed * piece, 8), piece)]
            for k, (_, arrive) in enumerate(z_copies[m]):
                arrive()
                total = total + z_in[m, k]
            gather[2 * m + core, own] = probe[m, core, own] + total * (1.0 / divisor)
            mine = gather.at[2 * m + core, own]
            group = [remote(mine, mine, dev) for dev in z_peers]
            for start, _ in group:
                start()
            z_back.append(group)
        for m in (0, 1):
            for _, arrive in z_back[m]:
                arrive()
            mine = gather.at[2 * m + core, pl.ds(pl.multiple_of(row_base, 8), part)]
            group = [remote(mine, mine, dev) for dev in row_peers]
            for start, _ in group:
                start()
            row_back.append(group)
    else:
        relay()

    a_so()
    a_dm()
    a_de()
    obj_out[:, top, :] = n1[:, top, 0:tile_cols] + from_up[...]
    obj_out[:, HALO:ODD_LOW, :] = n1[:, HALO:ODD_LOW, 0:tile_cols]
    obj_out[:, late, edge] = n1[:, late, edge] + (g1[:, 0:odd_own, edge] + spill1[:, 0:odd_own])
    obj_out[:, late, mid] = n1[:, late, mid] + g1[:, 0:odd_own, mid]

    if reduce_here:
        for m in (0, 1):
            for _, arrive in row_back[m]:
                arrive()
            mine = gather.at[2 * m + core]
            start, arrive = remote(mine, mine, partner)
            start()
            core_back.append(arrive)
        for m in (0, 1):
            core_back[m]()
            for p in (0, 1):
                probe_out[m, p] = gather[2 * m + p]
    else:
        for m in (0, 1):
            for p in (0, 1):
                probe_out[m, p] = sbuf[2 * m + p]

    for sends, copy in pending:
        if sends is None:
            copy.wait_send()
        else:
            pl.when(sends)(copy.wait_send)


def local(object_field, probe_modes, scan_positions, amplitudes):
    n_row, n_col = lax.axis_size("row"), lax.axis_size("col")
    width = probe_modes.shape[-1]
    _, tile_rows, tile_cols = object_field.shape
    batches = scan_positions.shape[2]
    divisor = math.sqrt(n_row * n_col * batches)
    lanes = tile_cols + HALO
    odd_rows = tile_rows - ODD_LOW + HALO
    n_zed = n_col // 2
    reduce_here = width % (n_row * n_zed * 8) == 0
    part = width // n_row
    piece = max(part // n_zed, 8)
    copies = 64 + 4 * (n_row + n_zed)
    vmem = pltpu.VMEM
    scratch = [
        vmem((2, tile_rows, lanes), F32),
        vmem((2, tile_rows, lanes), F32),
        vmem((2, tile_rows, lanes), F32),
        vmem((2, odd_rows, lanes), F32),
        vmem((2, odd_rows, lanes), F32),
        vmem((2, width, width), F32),
        vmem((2, tile_rows, HALO), F32),
        vmem((2, tile_rows, HALO), F32),
        vmem((2, odd_rows, HALO), F32),
        vmem((2, HALO, HALO), F32),
        vmem((2, HALO, tile_cols), F32),
    ]
    scratch += [vmem((2 * width, 2 * width), BF16) for _ in range(8)]
    scratch += [
        vmem((2, width, 2 * width), F32),
        vmem((2, width, width), F32),
        vmem((4, width, width), F32),
        vmem((2, width, width), F32),
        vmem((2, width, width), F32),
        vmem((2, n_row - 1, part, width), F32),
        vmem((2, part, width), F32),
        vmem((2, n_zed - 1, piece, width), F32),
        vmem((4, width, width), F32),
        pltpu.SemaphoreType.DMA((copies,)),
        pltpu.SemaphoreType.DMA((copies,)),
    ]
    whole = pl.BlockSpec(memory_space=pltpu.VMEM)
    object_out, probe_out = pl.pallas_call(
        functools.partial(kernel, n_row, n_col, reduce_here, divisor),
        out_shape=(
            jax.ShapeDtypeStruct(object_field.shape, F32),
            jax.ShapeDtypeStruct(probe_modes.shape, F32)),
        in_specs=[pl.BlockSpec(memory_space=pltpu.SMEM)] + [whole] * 4,
        out_specs=(whole, whole),
        scratch_shapes=scratch,
        compiler_params=pltpu.CompilerParams(
            collective_id=0, has_side_effects=True, vmem_limit_bytes=48 * 1024 * 1024),
        name="ptycho",
    )(
        scan_positions.reshape(-1), object_field, probe_modes,
        amplitudes.reshape(batches, width, width), jnp.asarray(dft_tables(width)))
    if not reduce_here:
        probe_out = probe_modes + lax.psum(probe_out, ("row", "col")) / divisor
    return object_out, probe_out


def solution(mesh):
    placed = (
        P(None, "row", "col"),
        P(),
        P("row", "col", None, None),
        P("row", "col", None, None, None),
    )
    return jax.shard_map(
        local, mesh=mesh, in_specs=placed, out_specs=(P(None, "row", "col"), P()), check_vma=False
    )
```

```python
import functools
import math

import jax
import jax.numpy as jnp
import numpy as np
from jax import lax
from jax.experimental import pallas as pl
from jax.experimental.pallas import tpu as pltpu
from jax.sharding import PartitionSpec as P

HALO = 128
ODD_LOW = 192
F32 = jnp.float32
BF16 = jnp.bfloat16
MESH = pl.DeviceIdType.MESH


def dft_tables(width):
    index = np.arange(width)
    angle = (index[:, None] * index[None, :] % width) * (2.0 * math.pi / width)
    out = []
    for table in (np.cos(angle) / math.sqrt(width), np.sin(angle) / math.sqrt(width)):
        table = table.astype(np.float32)
        high = table.astype(BF16)
        low = (table - high.astype(np.float32)).astype(BF16)
        out += [high, low]
    return np.stack(out)


def split(value):
    high = value.astype(BF16)
    return high, (value - high.astype(F32)).astype(BF16)


def dot3(a_hi, a_lo, b_hi, b_lo):
    dot = functools.partial(jnp.dot, preferred_element_type=F32)
    return dot(a_hi, b_hi) + (dot(a_hi, b_lo) + dot(a_lo, b_hi))


def kernel(
    n_row, n_col, reduce_here, divisor,
    pos, obj, probe_in, amps_in, tables_in, obj_hbm, probe_hbm,
    probe, amps, tables, obj_out, lsem,
    e0, gx, n1, e1, g1, zbuf, from_left, from_right, spill1, down_send, from_up,
    a_hi, a_lo, b_hi, b_lo, xs_hi, xs_lo, ls_hi, ls_lo, fbuf, wbuf,
    sbuf, core_in, tbuf, row_in, ubuf, z_in, gather, ssem, rsem,
):
    row = lax.axis_index("row")
    col = lax.axis_index("col")
    width = probe.shape[-1]
    tile_rows, tile_cols = obj.shape[1], obj.shape[2]
    odd_own = tile_rows - ODD_LOW
    core = lax.rem(col, 2)
    zed = col // 2
    n_zed = n_col // 2
    has_left, has_right = col > 0, col < n_col - 1
    has_up, has_down = row > 0, row < n_row - 1
    partner = (row, col + 1 - 2 * core)
    row_peers = [(lax.rem(row + k, n_row), col) for k in range(1, n_row)]
    z_peers = [(row, lax.rem(zed + k, n_zed) * 2 + core) for k in range(1, n_zed)]
    left, right = (row, col - 1), (row, col + 1)
    up, down = (row - 1, col), (row + 1, col)

    count = [0]
    pending = []

    def remote(src, dst, dev, sends=None, receives=None):
        i = count[0]
        count[0] += 1
        copy = pltpu.make_async_remote_copy(
            src_ref=src, dst_ref=dst, send_sem=ssem.at[i], recv_sem=rsem.at[i],
            device_id=dev, device_id_type=MESH)

        def start():
            if sends is None:
                copy.start()
            else:
                pl.when(sends)(copy.start)
            pending.append((sends, copy))

        def arrive():
            if receives is None:
                copy.wait_recv()
            else:
                pl.when(receives)(copy.wait_recv)

        return start, arrive

    fetches = [
        pltpu.make_async_copy(src, dst, lsem.at[i])
        for i, (src, dst) in enumerate((
            (tables_in, tables), (obj, e0.at[:, :, 0:tile_cols]), (probe_in, probe), (amps_in, amps)))]
    for fetch in fetches:
        fetch.start()

    barrier = pltpu.get_barrier_semaphore()
    beside = (row, lax.rem(col + 2 * core - 1 + n_col, n_col))
    greeted = [partner, beside] + row_peers + z_peers
    for dev in greeted:
        pl.semaphore_signal(barrier, inc=1, device_id=dev, device_id_type=MESH)
    pl.semaphore_wait(barrier, len(greeted))

    halo = slice(tile_cols, tile_cols + HALO)
    start, halo_arrives = remote(obj.at[:, :, 0:HALO], e0.at[:, 0:tile_rows, halo], left, has_left, has_right)
    start()

    fetches[0].wait()
    for hi, part in ((True, 0), (False, 1)):
        cosine, sine = tables[part], tables[2 + part]
        a, b = (a_hi, b_hi) if hi else (a_lo, b_lo)
        for i in (0, 1):
            a[pl.ds(i * width, width), pl.ds(i * width, width)] = cosine
            b[pl.ds(i * width, width), pl.ds(i * width, width)] = cosine
        a[0:width, width:] = sine
        a[width:, 0:width] = -sine
        b[0:width, width:] = -sine
        b[width:, 0:width] = sine
    fetches[2].wait()
    power = jnp.sum(
        jnp.sum(probe[0, 0] ** 2 + probe[0, 1] ** 2 + probe[1, 0] ** 2 + probe[1, 1] ** 2,
                axis=0, keepdims=True), axis=1, keepdims=True) / (width * width)
    step = 1.0 / (power + 1e-06)

    @pl.when(jnp.logical_not(has_right))
    def _():
        e0[:, 0:tile_rows, halo] = jnp.zeros((2, tile_rows, HALO), F32)
        from_right[...] = jnp.zeros_like(from_right)

    @pl.when(jnp.logical_not(has_left))
    def _():
        from_left[...] = jnp.zeros_like(from_left)
        spill1[...] = jnp.zeros_like(spill1)

    @pl.when(jnp.logical_not(has_down))
    def _():
        e1[:, odd_own : odd_own + HALO, :] = jnp.zeros((2, HALO, tile_cols + HALO), F32)

    @pl.when(jnp.logical_not(has_up))
    def _():
        from_up[...] = jnp.zeros_like(from_up)

    def block(i):
        return slice(i * width, (i + 1) * width)

    def one_hot(shape, dim, shift):
        here = lax.broadcasted_iota(jnp.int32, shape, dim)
        other = lax.broadcasted_iota(jnp.int32, shape, 1 - dim)
        return jnp.where(here == other + shift, 1.0, 0.0).astype(BF16)

    def pick(value, row_table, col_table):
        dot = functools.partial(jnp.dot, preferred_element_type=F32)
        parts = [dot(row_table, part).astype(BF16) for part in split(value)]
        return dot(parts[0], col_table) + dot(parts[1], col_table)

    def fit(source, first_row, col_start, batch, after_mode):
        height, total_lanes = source.shape[1:]
        row_table = one_hot((width, height), 1, first_row)
        col_table = one_hot((total_lanes, width), 0, col_start)
        for p in (0, 1):
            wbuf[p] = pick(source[p], row_table, col_table)
        for m in (0, 1):
            pr, pi, wr, wi = probe[m, 0], probe[m, 1], wbuf[0], wbuf[1]
            xs_hi[block(m), block(0)], xs_lo[block(m), block(0)] = split(pr * wr - pi * wi)
            xs_hi[block(m), block(1)], xs_lo[block(m), block(1)] = split(pr * wi + pi * wr)
        for m in (0, 1):
            y = dot3(xs_hi[block(m), :], xs_lo[block(m), :], b_hi[...], b_lo[...])
            for p in (0, 1):
                ls_hi[block(p), block(m)], ls_lo[block(p), block(m)] = split(y[:, block(p)])
        for p in (0, 1):
            fbuf[p] = dot3(a_hi[block(p), :], a_lo[block(p), :], ls_hi[...], ls_lo[...])
        intensity = sum(fbuf[p, :, block(m)] ** 2 for p in (0, 1) for m in (0, 1))
        factor = amps[batch].astype(F32) * lax.rsqrt(jnp.maximum(intensity, 0.1)) - 1.0
        for p in (0, 1):
            for m in (0, 1):
                ls_hi[block(p), block(m)], ls_lo[block(p), block(m)] = split(
                    fbuf[p, :, block(m)] * factor)
        for p in (0, 1):
            h = dot3(b_hi[block(p), :], b_lo[block(p), :], ls_hi[...], ls_lo[...])
            for m in (0, 1):
                xs_hi[block(m), block(p)], xs_lo[block(m), block(p)] = split(h[:, block(m)])
        for m in (0, 1):
            chi = dot3(xs_hi[block(m), :], xs_lo[block(m), :], a_hi[...], a_lo[...])
            cr, ci = chi[:, block(0)], chi[:, block(1)]
            pr, pi = probe[m, 0], probe[m, 1]
            gor, goi = (pr * cr + pi * ci) * step, (pr * ci - pi * cr) * step
            if m == 0:
                zbuf[0], zbuf[1] = gor, goi
            else:
                zbuf[0] += gor
                zbuf[1] += goi
            if batch == 0:
                fbuf[m] = chi
            else:
                probe_terms(chi, m, True)
                after_mode(m)

    def probe_terms(chi, m, more):
        cr, ci = chi[:, block(0)], chi[:, block(1)]
        wr, wi = wbuf[0], wbuf[1]
        terms = (wr * cr + wi * ci, wr * ci - wi * cr)
        for p in (0, 1):
            sbuf[2 * m + p] = sbuf[2 * m + p] + terms[p] if more else terms[p]

    def place(target, offset, col_start):
        height, total_lanes = target.shape[1:]
        row_table = one_hot((height, width), 0, offset)
        col_table = one_hot((width, total_lanes), 1, col_start)
        for p in (0, 1):
            target[p] = pick(zbuf[p], row_table, col_table)

    fetches[1].wait()
    fetches[3].wait()
    halo_arrives()
    fit(e0, pos[0, 0, 0, 0], pos[0, 0, 0, 1], 0, lambda m: None)
    place(gx, pos[0, 0, 0, 0], pos[0, 0, 0, 1])

    top, rest, late = slice(0, HALO), slice(HALO, tile_rows), slice(ODD_LOW, tile_rows)
    edge, mid = slice(0, HALO), slice(HALO, tile_cols)
    below = slice(odd_own, odd_own + HALO)
    s_rt, a_rt = remote(gx.at[:, top, halo], from_left.at[:, top], right, has_right, has_left)
    s_lt, a_lt = remote(gx.at[:, top, edge], from_right.at[:, top], left, has_left, has_right)
    s_rr, a_rr = remote(gx.at[:, rest, halo], from_left.at[:, rest], right, has_right, has_left)
    s_lr, a_lr = remote(gx.at[:, late, edge], from_right.at[:, late], left, has_left, has_right)
    s_um, a_um = remote(n1.at[:, top, mid], e1.at[:, below, mid], up, has_up, has_down)
    s_ue, a_ue = remote(n1.at[:, top, edge], e1.at[:, below, edge], up, has_up, has_down)
    s_uh, a_uh = remote(n1.at[:, top, halo], e1.at[:, below, halo], up, has_up, has_down)
    s_rt()
    s_lt()
    s_rr()
    s_lr()
    n1[:, top, mid] = e0[:, top, mid] + gx[:, top, mid]
    s_um()
    for m in (0, 1):
        probe_terms(fbuf[m], m, False)
    n1[:, rest, mid] = e0[:, rest, mid] + gx[:, rest, mid]
    inside = jnp.where(has_right, 1.0, 0.0).astype(F32)
    a_rt()
    n1[:, top, edge] = e0[:, top, edge] + gx[:, top, edge] + from_left[:, top]
    s_ue()
    a_lt()
    n1[:, top, halo] = (e0[:, top, halo] + gx[:, top, halo] + from_right[:, top]) * inside
    s_uh()
    a_rr()
    n1[:, rest, edge] = e0[:, rest, edge] + gx[:, rest, edge] + from_left[:, rest]
    a_lr()
    e1[:, 0:odd_own, 0:tile_cols] = n1[:, late, 0:tile_cols]
    e1[:, 0:odd_own, halo] = (e0[:, late, halo] + gx[:, late, halo] + from_right[:, late]) * inside
    a_um()
    a_ue()
    a_uh()

    core_copies = [
        remote(sbuf.at[2 * m + 1 - core], core_in.at[m], partner)
        for m in (0, 1) if reduce_here]

    def after_mode(m):
        if reduce_here:
            core_copies[m][0]()

    fit(e1, pos[0, 0, 1, 0] - ODD_LOW, pos[0, 0, 1, 1], 1, after_mode)
    place(g1, pos[0, 0, 1, 0] - ODD_LOW, pos[0, 0, 1, 1])

    s_sb, a_sb = remote(g1.at[:, below, halo], spill1.at[:, below], right, has_right, has_left)
    s_so, a_so = remote(g1.at[:, 0:odd_own, halo], spill1.at[:, 0:odd_own], right, has_right, has_left)
    s_dm, a_dm = remote(g1.at[:, below, mid], from_up.at[:, :, mid], down, has_down, has_up)
    s_de, a_de = remote(down_send, from_up.at[:, :, edge], down, has_down, has_up)
    s_sb()
    s_so()

    def relay():
        s_dm()
        a_sb()
        down_send[...] = g1[:, below, edge] + spill1[:, below]
        s_de()

    if reduce_here:
        part = width // n_row
        piece = part // n_zed
        row_base = row * part
        z_base = row_base + zed * piece
        row_copies, z_copies = [], []
        for m in (0, 1):
            core_copies[m][1]()
            tbuf[m] = sbuf[2 * m + core] + core_in[m]
            group = [
                remote(tbuf.at[m, pl.ds(pl.multiple_of(dev[0] * part, 8), part)], row_in.at[m, k], dev)
                for k, dev in enumerate(row_peers)]
            for start, _ in group:
                start()
            row_copies.append(group)
        relay()
        for m in (0, 1):
            total = tbuf[m, pl.ds(pl.multiple_of(row_base, 8), part)]
            for k, (_, arrive) in enumerate(row_copies[m]):
                arrive()
                total = total + row_in[m, k]
            ubuf[m] = total
            group = [
                remote(ubuf.at[m, pl.ds(pl.multiple_of(dev[1] // 2 * piece, 8), piece)], z_in.at[m, k], dev)
                for k, dev in enumerate(z_peers)]
            for start, _ in group:
                start()
            z_copies.append(group)
        z_back, row_back, core_back = [], [], []
        own = pl.ds(pl.multiple_of(z_base, 8), piece)
        for m in (0, 1):
            total = ubuf[m, pl.ds(pl.multiple_of(zed * piece, 8), piece)]
            for k, (_, arrive) in enumerate(z_copies[m]):
                arrive()
                total = total + z_in[m, k]
            gather[2 * m + core, own] = probe[m, core, own] + total * (1.0 / divisor)
            mine = gather.at[2 * m + core, own]
            group = [remote(mine, mine, dev) for dev in z_peers]
            for start, _ in group:
                start()
            z_back.append(group)
        for m in (0, 1):
            for _, arrive in z_back[m]:
                arrive()
            mine = gather.at[2 * m + core, pl.ds(pl.multiple_of(row_base, 8), part)]
            group = [remote(mine, mine, dev) for dev in row_peers]
            for start, _ in group:
                start()
            row_back.append(group)
    else:
        relay()

    a_so()
    a_dm()
    a_de()
    obj_out[:, top, :] = n1[:, top, 0:tile_cols] + from_up[...]
    obj_out[:, HALO:ODD_LOW, :] = n1[:, HALO:ODD_LOW, 0:tile_cols]
    obj_out[:, late, edge] = n1[:, late, edge] + (g1[:, 0:odd_own, edge] + spill1[:, 0:odd_own])
    obj_out[:, late, mid] = n1[:, late, mid] + g1[:, 0:odd_own, mid]
    stores = [pltpu.make_async_copy(obj_out, obj_hbm, lsem.at[len(fetches)])]
    stores[0].start()

    if reduce_here:
        for m in (0, 1):
            for _, arrive in row_back[m]:
                arrive()
            mine = gather.at[2 * m + core]
            start, arrive = remote(mine, mine, partner)
            start()
            core_back.append(arrive)
        for m in (0, 1):
            core_back[m]()
            stores.append(pltpu.make_async_copy(
                gather.at[pl.ds(2 * m, 2)], probe_hbm.at[m], lsem.at[len(fetches) + 1 + m]))
            stores[-1].start()
    else:
        for m in (0, 1):
            stores.append(pltpu.make_async_copy(
                sbuf.at[pl.ds(2 * m, 2)], probe_hbm.at[m], lsem.at[len(fetches) + 1 + m]))
            stores[-1].start()

    for store in stores:
        store.wait()
    for sends, copy in pending:
        if sends is None:
            copy.wait_send()
        else:
            pl.when(sends)(copy.wait_send)


def local(object_field, probe_modes, scan_positions, amplitudes):
    n_row, n_col = lax.axis_size("row"), lax.axis_size("col")
    width = probe_modes.shape[-1]
    _, tile_rows, tile_cols = object_field.shape
    batches = scan_positions.shape[2]
    divisor = math.sqrt(n_row * n_col * batches)
    lanes = tile_cols + HALO
    odd_rows = tile_rows - ODD_LOW + HALO
    n_zed = n_col // 2
    reduce_here = width % (n_row * n_zed * 8) == 0
    part = width // n_row
    piece = max(part // n_zed, 8)
    copies = 64 + 4 * (n_row + n_zed)
    vmem = pltpu.VMEM
    scratch = [
        vmem(probe_modes.shape, F32),
        vmem((batches, width, width), amplitudes.dtype),
        vmem((4, width, width), BF16),
        vmem(object_field.shape, F32),
        pltpu.SemaphoreType.DMA((8,)),
        vmem((2, tile_rows, lanes), F32),
        vmem((2, tile_rows, lanes), F32),
        vmem((2, tile_rows, lanes), F32),
        vmem((2, odd_rows, lanes), F32),
        vmem((2, odd_rows, lanes), F32),
        vmem((2, width, width), F32),
        vmem((2, tile_rows, HALO), F32),
        vmem((2, tile_rows, HALO), F32),
        vmem((2, odd_rows, HALO), F32),
        vmem((2, HALO, HALO), F32),
        vmem((2, HALO, tile_cols), F32),
    ]
    scratch += [vmem((2 * width, 2 * width), BF16) for _ in range(8)]
    scratch += [
        vmem((2, width, 2 * width), F32),
        vmem((2, width, width), F32),
        vmem((4, width, width), F32),
        vmem((2, width, width), F32),
        vmem((2, width, width), F32),
        vmem((2, n_row - 1, part, width), F32),
        vmem((2, part, width), F32),
        vmem((2, n_zed - 1, piece, width), F32),
        vmem((4, width, width), F32),
        pltpu.SemaphoreType.DMA((copies,)),
        pltpu.SemaphoreType.DMA((copies,)),
    ]
    whole = pl.BlockSpec(memory_space=pltpu.HBM)
    object_out, probe_out = pl.pallas_call(
        functools.partial(kernel, n_row, n_col, reduce_here, divisor),
        out_shape=(
            jax.ShapeDtypeStruct(object_field.shape, F32),
            jax.ShapeDtypeStruct(probe_modes.shape, F32)),
        in_specs=[pl.BlockSpec(memory_space=pltpu.SMEM)] + [whole] * 4,
        out_specs=(whole, whole),
        scratch_shapes=scratch,
        compiler_params=pltpu.CompilerParams(
            collective_id=0, has_side_effects=True, vmem_limit_bytes=64 * 1024 * 1024 - 128 * 1024),
        name="ptycho",
    )(
        scan_positions, object_field, probe_modes,
        amplitudes.reshape(batches, width, width), jnp.asarray(dft_tables(width)))
    if not reduce_here:
        probe_out = probe_modes + lax.psum(probe_out, ("row", "col")) / divisor
    return object_out, probe_out


def solution(mesh):
    placed = (
        P(None, "row", "col"),
        P(),
        P("row", "col", None, None),
        P("row", "col", None, None, None),
    )
    return jax.shard_map(
        local, mesh=mesh, in_specs=placed, out_specs=(P(None, "row", "col"), P()), check_vma=False
    )
```
